32 devices in a mesh: groups: 2 (over y), gx: 4 (over z), gy: 2 (over x), ta: 2 (over core).
Axes of the slice: x: 2, y: 2, z: 4, core: 2. Of those that a mesh axis runs over, the one named last changes fastest.
Arguments:
- field: bfloat16 [8, 16, 128, 128, 128], P(('groups', 'ta'), None, 'gx', 'gy'), parts along dimension 0, may hold values from -6 to 6
- bypass_weight: bfloat16 [16, 16], replicated, may hold values from -1.5 to 1.5
- bypass_bias: float32 [16], replicated, may hold values from -3 to 3
- spectral_weight: float32 [96, 24, 24, 2, 16, 16], P('gx', 'gy', 'ta'), may hold values from -6 to 6
Outputs:
- plume_state: bfloat16 [8, 16, 128, 128, 128], P(('groups', 'ta'), None, 'gx', 'gy'), parts along dimension 0
The draws below stay inside these ranges and needn't reach their ends.
There are 2 independent parts, one for each index of `groups`. The reference program is written for one: setup_inputs(seed, part) draws one part's arguments, and reference() takes and returns one part's arrays. A program takes and returns all parts, laid end to end along the dimension named above; an argument that names none is the same for every part. Nothing has to cross between parts.
All inputs are finite; a program needn't handle non-finite values.
Results may differ from the reference program's by a relative error of at most 0.001.
Values sent between devices are 32-bit elements; how exact they have to be, the bound alone decides.
A program may use at most 448 MiB of HBM per device.

```python
import math
import jax
import jax.numpy as jnp
from jax import lax

C = 16
NX = 128
NY = 128
NZ = 128
TW = 4
KX = 24
KY = 24
KZ = 24
KT = 4


def levels(rng, dims, split, smallest, top_value):
    level, own = 1.0, jax.random.fold_in(rng, 6)
    for position, blocks in split:
        heights = jnp.exp(jax.random.uniform(jax.random.fold_in(own, position), (blocks,), jnp.float32, smallest / len(split), top_value / len(split)))
        level = level * jnp.repeat(heights, dims[position] // blocks).reshape([-1 if axis == position else 1 for axis in range(len(dims))])
    return level


def noise(key, shape, spread, limit, pieces=(), kind=jnp.bfloat16):
    values = jax.random.normal(key, shape, jnp.float32) * spread
    if len(pieces) > 0:
        values = levels(key, shape, pieces, -0.22, 0.18) * values
    return jnp.clip(values, min=-limit, max=limit).astype(kind)


def setup_inputs(seed: int = 0, part: int = 0) -> dict:
    splits = jax.random.split(jax.random.key(seed), 5)
    part_splits = jax.random.split(jax.random.fold_in(splits[4], part), 5)
    field = noise(part_splits[0], (TW, C, NX, NY, NZ), 1.0, 6.0, ((0, 2), (2, 4), (3, 2)))
    bypass_weight = noise(splits[1], (C, C), C ** -0.5, 1.5)
    bypass_bias = noise(splits[2], (C,), 0.5, 3.0, (), jnp.float32)
    spectral_weight = noise(splits[3], (KT * KX, KY, KZ, 2, C, C), ((NX * NY * NZ * TW / (2 * C * KX * KY * KZ * KT)) ** 0.5), 6.0, ((0, 4), (1, 2), (2, 2)), jnp.float32)
    return {"field": field, "bypass_weight": bypass_weight, "bypass_bias": bypass_bias, "spectral_weight": spectral_weight}


full_turn = 2.0 * math.pi


def kept_freq(modes, length):
    positions = jnp.arange(modes, dtype=jnp.int32)
    return jnp.where(positions < modes // 2, positions, positions - modes + length).astype(jnp.int32)


def phase_angle(first_index, second_index, length):
    product = (first_index[:, None] * second_index[None, :]) % length
    return product.astype(jnp.float32) * (full_turn / length)


def block_table(first_index, second_index, length, orient):
    angle = phase_angle(first_index, second_index, length)
    cosine = jnp.cos(angle)
    sine = orient * jnp.sin(angle)
    real_row = jnp.stack([cosine, -sine], axis=-1)
    imag_row = jnp.stack([sine, cosine], axis=-1)
    return jnp.stack([real_row, imag_row], axis=1)


def apply_table(values, axis_freq, axis_part, phase_table):
    return jnp.tensordot(values, phase_table, axes=((axis_freq, axis_part), (0, 1)), precision=lax.Precision.HIGHEST)


def contract(values, weights):
    return jnp.einsum("abzi,abzio->abzo", values, weights, precision=lax.Precision.HIGHEST)


def reference(field, bypass_weight, bypass_bias, spectral_weight):
    z_angle = phase_angle(jnp.arange(NZ, dtype=jnp.int32), jnp.arange(KZ, dtype=jnp.int32), NZ)
    z_table = jnp.concatenate([jnp.cos(z_angle), -jnp.sin(z_angle)], axis=1)

    def forward_z(slab):
        flat = jnp.dot(slab.astype(jnp.float32).reshape(-1, NZ), z_table, precision=lax.Precision.HIGHEST)
        return flat.reshape(C, NX, NY, 2, KZ)

    spectrum = lax.map(forward_z, field)
    t_table = block_table(jnp.arange(TW, dtype=jnp.int32), kept_freq(KT, TW), TW, 1.0)
    x_table = block_table(jnp.arange(NX, dtype=jnp.int32), kept_freq(KX, NX), NX, 1.0)
    y_table = block_table(jnp.arange(NY, dtype=jnp.int32), kept_freq(KY, NY), NY, 1.0)
    in_t = apply_table(spectrum, 0, 4, t_table)
    in_x = apply_table(in_t, 1, 5, x_table)
    in_y = apply_table(in_x, 1, 5, y_table)
    modes = jnp.transpose(in_y, (2, 3, 4, 1, 5, 0)).reshape(KT * KX, KY, KZ, 2, C)
    real_in = modes[:, :, :, 0, :]
    imag_in = modes[:, :, :, 1, :]
    weight_real = spectral_weight[:, :, :, 0]
    weight_imag = spectral_weight[:, :, :, 1]
    mixed_real = contract(real_in, weight_real) - contract(imag_in, weight_imag)
    mixed_imag = contract(real_in, weight_imag) + contract(imag_in, weight_real)
    mixed = jnp.stack([mixed_real, mixed_imag], axis=3).reshape(KT, KX, KY, KZ, 2, C)
    y_inverse = block_table(kept_freq(KY, NY), jnp.arange(NY, dtype=jnp.int32), NY, -1.0)
    x_inverse = block_table(kept_freq(KX, NX), jnp.arange(NX, dtype=jnp.int32), NX, -1.0)
    t_inverse = block_table(kept_freq(KT, TW), jnp.arange(TW, dtype=jnp.int32), TW, -1.0)
    back_y = apply_table(mixed, 2, 4, y_inverse)
    back_x = apply_table(back_y, 1, 5, x_inverse)
    back_t = apply_table(back_x, 0, 5, t_inverse)
    slabs = jnp.transpose(back_t, (4, 1, 3, 2, 5, 0))
    back_angle = phase_angle(jnp.arange(KZ, dtype=jnp.int32), jnp.arange(NZ, dtype=jnp.int32), NZ)
    z_weight = jnp.where(jnp.arange(KZ, dtype=jnp.int32) == 0, 1.0, 2.0).astype(jnp.float32) / float(NX * NY * NZ * TW)
    inverse_z = jnp.stack([z_weight[:, None] * jnp.cos(back_angle), -z_weight[:, None] * jnp.sin(back_angle)], axis=0)

    def finish(paired):
        slab_modes, slab_field = paired
        spectral = jnp.tensordot(slab_modes, inverse_z, axes=((3, 4), (0, 1)), precision=lax.Precision.HIGHEST)
        bypass = jnp.einsum("cxyz,co->oxyz", slab_field.astype(jnp.float32), bypass_weight.astype(jnp.float32), precision=lax.Precision.HIGHEST)
        total = spectral + bypass + bypass_bias[:, None, None, None]
        return jax.nn.gelu(total, approximate=False).astype(jnp.bfloat16)

    return lax.map(finish, (slabs, field))
```

```python
import jax
import jax.numpy as jnp
import ml_dtypes
import numpy as np
from jax import lax
from jax.sharding import PartitionSpec as P

KX = 24
KY = 24
KZ = 24
KT = 4
HIGH = lax.Precision.HIGH


def kept_freq(modes, length):
    positions = np.arange(modes)
    return np.where(positions < modes // 2, positions, positions - modes + length)


def block_table(first_index, second_index, length, orient):
    angle = (first_index[:, None] * second_index[None, :] % length) * (2.0 * np.pi / length)
    cosine = np.cos(angle)
    sine = orient * np.sin(angle)
    real_row = np.stack([cosine, -sine], axis=-1)
    imag_row = np.stack([sine, cosine], axis=-1)
    return np.stack([real_row, imag_row], axis=1)


def own_part(table, axis, axis_name, size):
    start = lax.axis_index(axis_name) * size
    return lax.dynamic_slice_in_dim(jnp.asarray(table), start, size, axis=axis)


def on_device(field, bypass_weight, bypass_bias, spectral_weight):
    time_local, channels, x_local, y_local, nz = field.shape
    size_x, size_y, size_t = lax.axis_size("gx"), lax.axis_size("gy"), lax.axis_size("ta")
    nx, ny, nt = x_local * size_x, y_local * size_y, time_local * size_t
    ktx_local = spectral_weight.shape[0]
    freq_x, freq_y, freq_t = kept_freq(KX, nx), kept_freq(KY, ny), kept_freq(KT, nt)
    freq_z = np.arange(KZ)

    y_full = block_table(np.arange(ny), freq_y, ny, 1.0)[:, 0].astype(np.float32)
    y_high = y_full.astype(ml_dtypes.bfloat16)
    y_low = (y_full - y_high.astype(np.float32)).astype(ml_dtypes.bfloat16)
    in_y = sum(
        jnp.einsum(
            "tcxyz,ykp->tcxpkz",
            field,
            own_part(piece, 0, "gy", y_local),
            preferred_element_type=jnp.float32,
        )
        for piece in (y_high, y_low)
    )
    x_full = block_table(np.arange(nx), freq_x, nx, 1.0).astype(np.float32)
    in_x = jnp.einsum(
        "tcxpkz,xpmq->tcmkqz", in_y, own_part(x_full, 0, "gx", x_local), precision=HIGH
    )
    z_table = block_table(np.arange(nz), freq_z, nz, 1.0).astype(np.float32)
    in_z = jnp.einsum("tcmkqz,zqnr->tcmkrn", in_x, z_table, precision=HIGH)

    whole_time = lax.all_to_all(in_z, "ta", split_axis=5, concat_axis=0, tiled=True)
    t_table = block_table(np.arange(nt), freq_t, nt, 1.0).astype(np.float32)
    in_t = jnp.einsum("tcmkrn,trqs->kqmnsc", whole_time, t_table, precision=HIGH)
    rest = in_t.shape[3:]
    in_t = in_t.reshape((size_y, KY // size_y, KT * KX) + rest)
    by_y = lax.all_to_all(in_t, "gy", split_axis=0, concat_axis=0, tiled=True).sum(0)
    by_y = jnp.swapaxes(by_y, 0, 1).reshape((size_x, ktx_local, KY // size_y) + rest)
    modes = lax.all_to_all(by_y, "gx", split_axis=0, concat_axis=0, tiled=True).sum(0)

    real_in, imag_in = modes[:, :, :, 0, :, None], modes[:, :, :, 1, :, None]
    weight_real, weight_imag = spectral_weight[:, :, :, 0], spectral_weight[:, :, :, 1]
    mixed_real = jnp.sum(real_in * weight_real - imag_in * weight_imag, axis=3)
    mixed_imag = jnp.sum(real_in * weight_imag + imag_in * weight_real, axis=3)
    mixed = jnp.stack([mixed_real, mixed_imag], axis=3)

    gathered = lax.all_gather(mixed, "gy", axis=1, tiled=True)
    gathered = lax.all_gather(gathered, "gx", axis=0, tiled=True)
    gathered = gathered.reshape((KT, KX) + gathered.shape[1:])
    t_inverse = block_table(freq_t, np.arange(nt), nt, -1.0).astype(np.float32)
    out_t = jnp.einsum("qmknso,qstr->tomkrn", gathered, t_inverse, precision=HIGH)
    own_time = lax.all_to_all(out_t, "ta", split_axis=0, concat_axis=5, tiled=True)
    z_weight = np.where(freq_z == 0, 1.0, 2.0) / float(nx * ny * nz * nt)
    z_inverse = block_table(freq_z, np.arange(nz), nz, -1.0) * z_weight[:, None, None, None]
    out_z = jnp.einsum(
        "tomkrn,nrzp->tomkpz", own_time, z_inverse.astype(np.float32), precision=HIGH
    )
    x_inverse = block_table(freq_x, np.arange(nx), nx, -1.0).astype(np.float32)
    out_x = jnp.einsum(
        "tomkpz,mpxq->toxkqz", out_z, own_part(x_inverse, 2, "gx", x_local), precision=HIGH
    )
    y_inverse = block_table(freq_y, np.arange(ny), ny, -1.0)[:, :, :, 0].astype(np.float32)
    spectral = jnp.einsum(
        "toxkqz,kqy->toxyz", out_x, own_part(y_inverse, 2, "gy", y_local), precision=HIGH
    )
    bypass = jnp.einsum("tcxyz,co->toxyz", field, bypass_weight, preferred_element_type=jnp.float32)
    total = spectral + bypass + bypass_bias[None, :, None, None, None]
    return jax.nn.gelu(total, approximate=False).astype(jnp.bfloat16)


def solution(mesh):
    in_specs = (
        P(("groups", "ta"), None, "gx", "gy", None),
        P(),
        P(),
        P("gx", "gy", "ta", None, None, None),
    )
    out_specs = P(("groups", "ta"), None, "gx", "gy", None)
    return jax.shard_map(
        on_device, mesh=mesh, in_specs=in_specs, out_specs=out_specs, check_vma=False
    )
```

```python
import jax
import jax.numpy as jnp
import ml_dtypes
import numpy as np
from jax import lax
from jax.sharding import PartitionSpec as P

KX = 24
KY = 24
KZ = 24
KT = 4
HIGH = lax.Precision.HIGH


def kept_freq(modes, length):
    positions = np.arange(modes)
    return np.where(positions < modes // 2, positions, positions - modes + length)


def block_table(first_index, second_index, length, orient):
    angle = (first_index[:, None] * second_index[None, :] % length) * (2.0 * np.pi / length)
    cosine = np.cos(angle)
    sine = orient * np.sin(angle)
    real_row = np.stack([cosine, -sine], axis=-1)
    imag_row = np.stack([sine, cosine], axis=-1)
    return np.stack([real_row, imag_row], axis=1)


def own_part(table, axis, axis_name, size):
    start = lax.axis_index(axis_name) * size
    return lax.dynamic_slice_in_dim(jnp.asarray(table), start, size, axis=axis)


def gather(block, axis_name, size):
    copies = jnp.broadcast_to(block[None], (size,) + block.shape)
    return lax.all_to_all(copies, axis_name, split_axis=0, concat_axis=0, tiled=True)


def on_device(field, bypass_weight, bypass_bias, spectral_weight):
    time_local, channels, x_local, y_local, nz = field.shape
    size_x, size_y, size_t = lax.axis_size("gx"), lax.axis_size("gy"), lax.axis_size("ta")
    nx, ny, nt = x_local * size_x, y_local * size_y, time_local * size_t
    ktx_local = spectral_weight.shape[0]
    freq_x, freq_y, freq_t = kept_freq(KX, nx), kept_freq(KY, ny), kept_freq(KT, nt)
    freq_z = np.arange(KZ)

    y_full = block_table(np.arange(ny), freq_y, ny, 1.0)[:, 0].astype(np.float32)
    y_high = y_full.astype(ml_dtypes.bfloat16)
    y_low = (y_full - y_high.astype(np.float32)).astype(ml_dtypes.bfloat16)
    in_y = sum(
        jnp.einsum(
            "tcxyz,ykp->tcxpkz",
            field,
            own_part(piece, 0, "gy", y_local),
            preferred_element_type=jnp.float32,
        )
        for piece in (y_high, y_low)
    )
    x_full = block_table(np.arange(nx), freq_x, nx, 1.0).astype(np.float32)
    in_x = jnp.einsum(
        "tcxpkz,xpmq->tckmqz", in_y, own_part(x_full, 0, "gx", x_local), precision=HIGH
    )
    z_table = block_table(np.arange(nz), freq_z, nz, 1.0).astype(np.float32)
    z_table = z_table.reshape(nz, 2, size_t, KZ // size_t, 2)
    in_x = in_x.reshape(time_local, channels, KY * KX, 2, nz)
    in_z = jnp.einsum("tcjqz,zqhnr->htrncj", in_x, z_table, precision=HIGH)

    whole_time = lax.all_to_all(in_z, "ta", split_axis=0, concat_axis=0, tiled=True)
    t_table = block_table(np.arange(nt), freq_t, nt, 1.0).astype(np.float32)
    t_table = t_table.reshape(size_t, time_local, 2, KT, 2)
    in_t = jnp.einsum("htrncj,htrqs->qnscj", whole_time, t_table, precision=HIGH)
    rest = in_t.shape[1:4]
    in_t = jnp.transpose(in_t.reshape((KT,) + rest + (KY, KX)), (4, 0, 5, 1, 2, 3))
    in_t = in_t.reshape((size_y, KY // size_y, KT * KX) + rest)
    by_y = lax.all_to_all(in_t, "gy", split_axis=0, concat_axis=0, tiled=True).sum(0)
    by_y = jnp.swapaxes(by_y, 0, 1).reshape((size_x, ktx_local, KY // size_y) + rest)
    modes = lax.all_to_all(by_y, "gx", split_axis=0, concat_axis=0, tiled=True).sum(0)

    real_in, imag_in = modes[:, :, :, 0, :, None], modes[:, :, :, 1, :, None]
    weight_real, weight_imag = spectral_weight[:, :, :, 0], spectral_weight[:, :, :, 1]
    mixed_real = jnp.sum(real_in * weight_real - imag_in * weight_imag, axis=3)
    mixed_imag = jnp.sum(real_in * weight_imag + imag_in * weight_real, axis=3)
    mixed = jnp.stack([mixed_real, mixed_imag], axis=3)

    gathered = gather(gather(mixed, "gx", size_x), "gy", size_y)
    gathered = gathered.reshape((size_y, KT, KX) + mixed.shape[1:])
    t_inverse = block_table(freq_t, np.arange(nt), nt, -1.0).astype(np.float32)
    t_inverse = t_inverse.reshape(KT, 2, size_t, time_local, 2)
    out_t = jnp.einsum("yqmbnso,qshtr->htrnoybm", gathered, t_inverse, precision=HIGH)
    out_t = out_t.reshape(out_t.shape[:5] + (KY * KX,))
    own_time = lax.all_to_all(out_t, "ta", split_axis=0, concat_axis=0, tiled=True)
    z_weight = np.where(freq_z == 0, 1.0, 2.0) / float(nx * ny * nz * nt)
    z_inverse = block_table(freq_z, np.arange(nz), nz, -1.0) * z_weight[:, None, None, None]
    z_inverse = z_inverse.astype(np.float32).reshape(size_t, KZ // size_t, 2, nz, 2)
    out_z = jnp.einsum("htrnoj,hnrzp->tojpz", own_time, z_inverse, precision=HIGH)
    out_z = out_z.reshape(time_local, channels, KY, KX, 2, nz)
    x_inverse = block_table(freq_x, np.arange(nx), nx, -1.0).astype(np.float32)
    out_x = jnp.einsum(
        "tokmpz,mpxq->toxkqz", out_z, own_part(x_inverse, 2, "gx", x_local), precision=HIGH
    )
    y_inverse = block_table(freq_y, np.arange(ny), ny, -1.0)[:, :, :, 0].astype(np.float32)
    spectral = jnp.einsum(
        "toxkqz,kqy->toxyz", out_x, own_part(y_inverse, 2, "gy", y_local), precision=HIGH
    )
    bypass = jnp.einsum("tcxyz,co->toxyz", field, bypass_weight, preferred_element_type=jnp.float32)
    total = spectral + bypass + bypass_bias[None, :, None, None, None]
    return jax.nn.gelu(total, approximate=False).astype(jnp.bfloat16)


def solution(mesh):
    in_specs = (
        P(("groups", "ta"), None, "gx", "gy", None),
        P(),
        P(),
        P("gx", "gy", "ta", None, None, None),
    )
    out_specs = P(("groups", "ta"), None, "gx", "gy", None)
    return jax.shard_map(
        on_device, mesh=mesh, in_specs=in_specs, out_specs=out_specs, check_vma=False
    )
```
